128 devices in a mesh: pool: 8 (over y, core), tp: 16 (over z, x).
Axes of the slice: x: 4, y: 4, z: 4, core: 2. Of those that a mesh axis runs over, the one named last changes fastest.
Arguments:
- queries: bfloat16 [64, 4, 24576], P('pool', None, 'tp'), may hold values from -18 to 18
- new_rows: bfloat16 [64, 4, 576], P('pool'), may hold values from -4 to 4
- prefill_latent: bfloat16 [8, 16, 44, 128, 512], P('pool', 'tp'), may hold values from -6 to 6
- prefill_rope: bfloat16 [8, 16, 44, 64, 128], P('pool', 'tp'), may hold values from -6 to 6
- lengths: int32 [8, 8], replicated, may hold values from 1 to 16384, 73728 in all within a row
- owner: int32 [8, 8], replicated, may hold values from 0 to 7, as said below
- pack_order: int32 [8, 16, 8], P('pool', 'tp'), may hold values from 0 to 7, each once within a row
- uk_weight: bfloat16 [128, 128, 512], P('tp'), may hold values from -0.5 to 0.5
- uv_weight: bfloat16 [128, 512, 128], P('tp'), may hold values from -1 to 1
- out_weight: bfloat16 [16384, 7168], P('tp'), may hold values from -0.1875 to 0.1875
Outputs:
- attended: bfloat16 [64, 4, 7168], P('pool')
The draws below stay inside these ranges and needn't reach their ends.
Inputs may be any that keep to these rules, and one draw needn't show every extreme that they name: For every k, owner[:, k] names each decode group once, and the 8 entries of each row of owner differ. Each pack_order[p, t] is a permutation of the 8 sequences of group p. Every row of lengths sums to 73728 and its largest entry is exactly 16384.
All inputs are finite; a program needn't handle non-finite values.
Results may differ from the reference program's by a relative error of at most 0.02.
Values may be sent and summed in bfloat16 or wider, within the bound.
A program may use at most 128 MiB of HBM per device.

```python
import math
import jax
import jax.numpy as jnp
import numpy as np
from jax import lax

D = 7168
HEADS = 128
NOPE = 128
ROPE = 64
KV_RANK = 512
VDIM = 128
STEPS = 4
BLK_ROWS = 128
MAXLEN = 16384
SEQ_GRP = 8
SEQS = 64
GROUP_LEN = 73728
PB = 44
N_POOL = 8
N_TP = 16


def draw_queries(key, part):
    key = jax.random.fold_in(key, 21)
    first_key = jax.random.fold_in(key, 0)
    row_width = NOPE + ROPE
    values = jnp.clip(jax.random.normal(first_key, (SEQS, STEPS, HEADS, row_width), jnp.float32), -4.0, 4.0)
    return values.reshape(SEQS, STEPS, HEADS * row_width).astype(jnp.bfloat16)


def draw_new_rows(key, part):
    key = jax.random.fold_in(key, 22)
    row_width = KV_RANK + ROPE
    values = jnp.clip(jax.random.normal(key, (SEQS, STEPS, row_width), jnp.float32), -4.0, 4.0)
    return values.astype(jnp.bfloat16)


def draw_prefill_rope(key, part):
    key = jax.random.fold_in(key, 23)
    full_shape = (N_POOL, N_TP, PB, ROPE, BLK_ROWS)
    values = jnp.clip(jax.random.normal(key, full_shape, jnp.float32), -6.0, 6.0)
    return values.astype(jnp.bfloat16)


def draw_owner(key, part):
    key = jax.random.fold_in(key, 31)
    first_key, second_key, third_key = jax.random.split(key, 3)
    relabel = jax.random.permutation(first_key, N_POOL)
    row_shift = jax.random.permutation(second_key, N_POOL)
    column_shift = jax.random.permutation(third_key, N_POOL)[:SEQ_GRP]
    combined = (row_shift[:, None] + column_shift[None, :]) % N_POOL
    return jnp.take(relabel, combined).astype(jnp.int32)


def block_levels(stream_key, dims, cuts, smallest, top_value):
    def one(axis_at, parts):
        draws = jax.random.uniform(jax.random.fold_in(jax.random.fold_in(stream_key, 6), axis_at), (parts,), jnp.float32, smallest / len(cuts), top_value / len(cuts))
        return jnp.repeat(jnp.exp(draws), dims[axis_at] // parts).reshape((-1,) + (1,) * (len(dims) - axis_at - 1))

    factor_of = one(*cuts[0])
    for cut in cuts[1:]:
        factor_of = factor_of * one(*cut)
    return factor_of


def split_up(number_of, total, most, lean):
    loads = [(1 << 20) // math.isqrt(grade ** lean) + 1 for grade in range(2, number_of + 1)]
    rest, given = total - most - (number_of - 1), [1] * (number_of - 1)
    while rest > 0:
        movable = [i for i in range(number_of - 1) if given[i] < most]
        whole, left = sum([loads[i] for i in movable]), rest
        for i in movable:
            more = min(most - given[i], max(1, left * loads[i] // whole), rest)
            given[i] = given[i] + more
            rest = rest - more
    return np.array([most] + given)


def ragged(stream_key, number_of, total, bound, lean):
    if number_of == 2:
        one = jax.random.randint(stream_key, (), max(1, total - bound), min(bound, total - 1) + 1)
        return jnp.stack([one, total - one])
    sizes = jnp.asarray(split_up(number_of, total, bound, lean), jnp.int32)
    twos = (number_of - 1) // 2
    giver, sink = sizes[1:1 + 2 * twos:2], sizes[2:2 + 2 * twos:2]
    room = jnp.minimum(giver - 1, bound - sink)
    moved = jax.random.randint(jax.random.fold_in(stream_key, 1), (twos,), 0, 1 << 20) % (room + 1)
    sizes = sizes.at[1:1 + 2 * twos:2].set(giver - moved).at[2:2 + 2 * twos:2].set(sink + moved)
    return sizes[jax.random.permutation(jax.random.fold_in(stream_key, 2), number_of)]


def normal_values(own_key, extent, width, bound, cuts=(), kind=jnp.bfloat16):
    values = width * jax.random.normal(own_key, extent, jnp.float32)
    if cuts:
        values = values * block_levels(own_key, extent, cuts, -0.22, 0.18)
    return jnp.clip(values, -bound, bound).astype(kind)


def setup_inputs(seed: int = 0) -> dict:
    key_list = jax.random.split(jax.random.key(seed), 11)
    queries = draw_queries(jax.random.fold_in(key_list[10], 71), 0)
    new_rows = draw_new_rows(jax.random.fold_in(key_list[10], 71), 0)
    prefill_latent = normal_values(key_list[2], (N_POOL, N_TP, PB, BLK_ROWS, KV_RANK), 1.0, 6.0, ((0, 8), (1, 16)))
    prefill_rope = draw_prefill_rope(jax.random.fold_in(key_list[10], 71), 0)
    lengths = jax.vmap(lambda own: ragged(own, SEQ_GRP, GROUP_LEN, MAXLEN, 2))(jax.random.split(key_list[4], N_POOL)).reshape((N_POOL, SEQ_GRP)).astype(jnp.int32)
    owner = draw_owner(jax.random.fold_in(key_list[10], 71), 0)
    pack_order = jax.vmap(lambda own: jax.random.permutation(own, SEQ_GRP))(jax.random.split(key_list[6], N_POOL * N_TP)).reshape((N_POOL, N_TP, SEQ_GRP)).astype(jnp.int32)
    uk_weight = normal_values(key_list[7], (HEADS, NOPE, KV_RANK), NOPE ** -0.5, 0.5, ((0, 16),))
    uv_weight = normal_values(key_list[8], (HEADS, KV_RANK, VDIM), (max(KV_RANK // 16, 1)) ** -0.5, 1.0, ((0, 16),))
    out_weight = normal_values(key_list[9], (HEADS * VDIM, D), (max(HEADS * VDIM // 16, 1)) ** -0.5, 0.1875, ((0, 16),))
    return dict(queries=queries, new_rows=new_rows, prefill_latent=prefill_latent, prefill_rope=prefill_rope, lengths=lengths, owner=owner, pack_order=pack_order, uk_weight=uk_weight, uv_weight=uv_weight, out_weight=out_weight)


MASKED = -1e30


def block_starts(lengths, pack_order):
    blocks = (lengths + BLK_ROWS - 1) // BLK_ROWS
    tensor_numbers = jnp.arange(N_TP, dtype=jnp.int32)
    counts = jnp.maximum(blocks[:, None, :] - tensor_numbers[None, :, None] + N_TP - 1, 0) // N_TP
    ordered = jnp.take_along_axis(counts, pack_order, axis=2)
    before = (jnp.cumsum(ordered, axis=2) - ordered).astype(jnp.int32)
    slot_numbers = jnp.arange(SEQ_GRP, dtype=jnp.int32)
    onehot = (pack_order[..., :, None] == slot_numbers[None, None, None, :]).astype(jnp.int32)
    return jnp.sum(onehot * before[..., None], axis=2).astype(jnp.int32)


def reference(queries, new_rows, prefill_latent, prefill_rope, lengths, owner, pack_order, uk_weight, uv_weight, out_weight):
    score_scale = (NOPE + ROPE) ** -0.5
    split_queries = queries.reshape(SEQS, STEPS, HEADS, NOPE + ROPE)
    absorbed = jnp.einsum('sihn,hnd->sihd', split_queries[..., :NOPE].astype(jnp.float32), uk_weight.astype(jnp.float32)).astype(jnp.bfloat16)
    rope_queries = split_queries[..., NOPE:]
    starts = block_starts(lengths, pack_order)
    group_numbers = jnp.arange(N_POOL, dtype=jnp.int32)
    matches = (owner[None, :, :] == group_numbers[:, None, None]).astype(jnp.int32)
    source_of = jnp.sum(matches * group_numbers[None, :, None], axis=1).astype(jnp.int32)
    block_slots = MAXLEN // (BLK_ROWS * N_TP)
    tensor_numbers = jnp.arange(N_TP, dtype=jnp.int32)
    slot_numbers = jnp.arange(block_slots, dtype=jnp.int32)
    positions = BLK_ROWS * (tensor_numbers[:, None, None] + N_TP * slot_numbers[None, :, None]) + jnp.arange(BLK_ROWS, dtype=jnp.int32)[None, None, :]
    step_numbers = jnp.arange(STEPS, dtype=jnp.int32)
    causal = (step_numbers[None, :] <= step_numbers[:, None])[:, None, :]

    def one_sequence(sequence):
        group_index = sequence // SEQ_GRP
        slot_index = sequence % SEQ_GRP
        source = source_of[group_index, slot_index]
        length = lengths[source, slot_index]
        first_block = starts[source, :, slot_index]
        block_index = jnp.minimum(first_block[:, None] + slot_numbers[None, :], PB - 1).astype(jnp.int32)
        latents = prefill_latent[source][tensor_numbers[:, None], block_index].astype(jnp.float32)
        rope_rows = prefill_rope[source][tensor_numbers[:, None], block_index].astype(jnp.float32)
        usable = positions < length
        query_latent = absorbed[sequence].astype(jnp.float32)
        query_rope = rope_queries[sequence].astype(jnp.float32)
        scores = (jnp.einsum('ihd,tcnd->ihtcn', query_latent, latents) + jnp.einsum('ihe,tcen->ihtcn', query_rope, rope_rows)) * score_scale
        fresh_rows = new_rows[sequence].astype(jnp.float32)
        fresh_scores = (jnp.einsum('ihd,jd->ihj', query_latent, fresh_rows[:, :KV_RANK]) + jnp.einsum('ihe,je->ihj', query_rope, fresh_rows[:, KV_RANK:])) * score_scale
        maxima = jnp.maximum(jnp.max(jnp.where(usable, scores, MASKED), axis=(2, 3, 4)), jnp.max(jnp.where(causal, fresh_scores, MASKED), axis=2))
        weights = jnp.where(usable, jnp.exp(scores - maxima[:, :, None, None, None]), 0.0)
        rounded = lax.optimization_barrier(weights.astype(jnp.bfloat16)).astype(jnp.float32)
        latent = jnp.einsum('ihtcn,tcnd->ihd', rounded, latents)
        totals = jnp.sum(weights, axis=(2, 3, 4))
        fresh_weights = jnp.where(causal, jnp.exp(fresh_scores - maxima[:, :, None]), 0.0)
        latent = latent + jnp.einsum('ihj,jd->ihd', fresh_weights, fresh_rows[:, :KV_RANK])
        totals = totals + jnp.sum(fresh_weights, axis=2)
        mixture = (latent / totals[..., None]).astype(jnp.bfloat16)
        values = jnp.einsum('ihd,hdv->ihv', mixture.astype(jnp.float32), uv_weight.astype(jnp.float32)).astype(jnp.bfloat16)
        return jnp.dot(values.reshape(STEPS, HEADS * VDIM), out_weight, preferred_element_type=jnp.float32).astype(jnp.bfloat16)

    return lax.map(one_sequence, jnp.arange(SEQS, dtype=jnp.int32))
```

```python
import jax
import jax.numpy as jnp
from jax import lax
from jax.experimental import pallas as pl
from jax.experimental.pallas import tpu as pltpu
from jax.sharding import PartitionSpec as P

MESH = pl.DeviceIdType.MESH
F32 = jnp.float32
BF16 = jnp.bfloat16
MASKED = -1e30

POOL = 8
SIDE = 4
TP = 16
SEQ = 8
STEPS = 4
HEADS = 8
NOPE = 128
ROPE = 64
RANK = 512
BLOCKS = 44
ROWS = 128
SLOTS = 8
KEYS = SLOTS * ROWS
SHARD = HEADS * STEPS
PACK = SHARD * 4 + SHARD // 2
WIDTH = 7168
CHUNK = 896
SCALE = (NOPE + ROPE) ** -0.5


def iota(shape, dim):
    return lax.broadcasted_iota(jnp.int32, shape, dim)


def dot(a, b):
    return jnp.dot(a, b, preferred_element_type=F32)


def dot_nt(a, b):
    return lax.dot_general(a, b, (((1,), (1,)), ((), ())), preferred_element_type=F32)


def two_columns(first, second):
    lane = iota((first.shape[0], 128), 1)
    return jnp.where(lane == 0, first, jnp.where(lane == 1, second, 0.0))


def merge(parts):
    top = parts[0][1]
    for part in parts[1:]:
        top = jnp.maximum(top, part[1])
    sums, totals = 0.0, 0.0
    for part in parts:
        factor = jnp.exp(part[1] - top)
        sums = sums + factor * part[0].astype(F32)
        totals = totals + factor * part[2]
    return sums, top, totals


def kernel(
    owner,
    lengths,
    packing,
    queries_hbm,
    fresh_hbm,
    latent_hbm,
    rope_hbm,
    uk_hbm,
    uv_hbm,
    out_weight_hbm,
    out_ref,
    queries,
    fresh,
    latents,
    ropes,
    uk,
    uv,
    out_weight,
    wide,
    absorbed,
    outgoing,
    gathered,
    keys,
    rope_keys,
    sums1,
    stats1,
    sums1_in,
    stats1_in,
    sums2,
    stats2,
    sums2_in,
    stats2_in,
    turned,
    sums3,
    stats3,
    sums3_in,
    stats3_in,
    fresh_sums,
    fresh_stats,
    part_out,
    part_in,
    local_sem,
    a2a_send,
    a2a_recv,
    ag1_send,
    ag1_recv,
    ag2_send,
    ag2_recv,
    rs1_send,
    rs1_recv,
    rs1s_send,
    rs1s_recv,
    rs2_send,
    rs2_recv,
    rs2s_send,
    rs2s_recv,
    ret_send,
    ret_recv,
    rets_send,
    rets_recv,
    fin_send,
    fin_recv,
    all_send,
    all_recv,
):
    pool = lax.axis_index("pool")
    tp = lax.axis_index("tp")
    z, x = tp // SIDE, tp % SIDE

    def load(index, source, target):
        return pltpu.make_async_copy(source, target, local_sem.at[index])

    loads = [
        load(0, queries_hbm, queries),
        load(1, uk_hbm, uk),
        load(2, fresh_hbm, fresh),
        load(3, latent_hbm, latents),
        load(4, rope_hbm, ropes),
    ]
    for h in range(HEADS):
        loads.append(load(5 + h, uv_hbm.at[h], uv.at[:, h * 128 : (h + 1) * 128]))
    loads.append(load(5 + HEADS, out_weight_hbm, out_weight))
    for copy in loads:
        copy.start()

    barrier = pltpu.get_barrier_semaphore()
    for j in range(1, POOL):
        pl.semaphore_signal(
            barrier, inc=1, device_id=((pool + j) % POOL, tp), device_id_type=MESH
        )
    for j in range(1, TP):
        pl.semaphore_signal(barrier, inc=1, device_id=(pool, (tp + j) % TP), device_id_type=MESH)

    def slot_of(s, g):
        slot = jnp.int32(0)
        for k in range(1, SEQ):
            slot = jnp.where(owner[s, k] == g, k, slot)
        return slot

    slots = [slot_of((pool + POOL - d) % POOL, pool) for d in range(SEQ)]

    def slot_vector(which):
        vector = jnp.zeros(which.shape, jnp.int32)
        for d in range(SEQ):
            vector = jnp.where(which == d, slots[d], vector)
        return vector

    wide[...] = jnp.zeros_like(wide)
    row, lane = iota((ROPE, 128), 0), iota((ROPE, 128), 1)
    unit = jnp.where((lane & (ROPE - 1)) == row, 1.0, 0.0).astype(BF16)
    for h in range(HEADS):
        start = h * (NOPE + ROPE)
        wide[start + NOPE : start + NOPE + ROPE, RANK:] = unit
    loads[1].wait()
    for h in range(HEADS):
        start = h * (NOPE + ROPE)
        wide[start : start + NOPE, :RANK] = uk[h]
    count = SEQ * SHARD
    row, col = iota((count, SEQ * STEPS), 0), iota((count, SEQ * STEPS), 1)
    pick = ((col >> 2) == slot_vector(row >> 5)) & ((col & 3) == (row & 3))
    loads[0].wait()
    spread = dot(jnp.where(pick, 1.0, 0.0).astype(BF16), queries[...])
    row, lane = iota(spread.shape, 0), iota(spread.shape, 1)
    first = ((row >> 2) & (HEADS - 1)) * (NOPE + ROPE)
    spread = jnp.where((lane >= first) & (lane < first + NOPE + ROPE), spread, 0.0)
    absorbed[...] = dot(spread.astype(BF16), wide[...]).astype(BF16)

    def place(par):
        return z + par * (x - z), x + par * (z - x)

    def minor_peer(par, j):
        major, minor = place(par)
        to = (minor + j) % SIDE
        return to, (pool, (1 - par) * (z * SIDE + to) + par * (to * SIDE + x))

    def major_peer(par, j):
        major, minor = place(par)
        to = (major + j) % SIDE
        return to, (pool, (1 - par) * (to * SIDE + x) + par * (z * SIDE + to))

    def remote(source, target, send, recv, device):
        return pltpu.make_async_remote_copy(
            src_ref=source,
            dst_ref=target,
            send_sem=send,
            recv_sem=recv,
            device_id=device,
            device_id_type=MESH,
        )

    def a2a(d):
        major, minor = place(d % 2)
        return remote(
            outgoing.at[d],
            gathered.at[d, major * SIDE + minor],
            a2a_send.at[d],
            a2a_recv.at[d],
            ((pool + POOL - d) % POOL, tp),
        )

    def ag1(d, j):
        major, minor = place(d % 2)
        piece = gathered.at[d, major * SIDE + minor]
        return remote(
            piece, piece, ag1_send.at[d, j], ag1_recv.at[d, j], minor_peer(d % 2, j + 1)[1]
        )

    def ag2(d, j):
        major, minor = place(d % 2)
        piece = gathered.at[d, pl.ds(major * SIDE, SIDE)]
        return remote(
            piece, piece, ag2_send.at[d, j], ag2_recv.at[d, j], major_peer(d % 2, j + 1)[1]
        )

    def rs1(d, j):
        to, device = major_peer(d % 2, j + 1)
        return (
            remote(
                sums1.at[d, pl.ds(to * SIDE, SIDE)],
                sums1_in.at[d, j],
                rs1_send.at[d, j],
                rs1_recv.at[d, j],
                device,
            ),
            remote(
                stats1.at[d, to],
                stats1_in.at[d, j],
                rs1s_send.at[d, j],
                rs1s_recv.at[d, j],
                device,
            ),
        )

    def rs2(d, j):
        to, device = minor_peer(d % 2, j + 1)
        return (
            remote(
                sums2.at[d, to],
                sums2_in.at[d, j],
                rs2_send.at[d, j],
                rs2_recv.at[d, j],
                device,
            ),
            remote(
                stats2.at[d],
                stats2_in.at[d, j],
                rs2s_send.at[d, j],
                rs2s_recv.at[d, j],
                device,
            ),
        )

    def back(d):
        device = ((pool + d) % POOL, tp)
        return (
            remote(sums3.at[d], sums3_in.at[d], ret_send.at[d], ret_recv.at[d], device),
            remote(stats3.at[d], stats3_in.at[d], rets_send.at[d], rets_recv.at[d], device),
        )

    def packed(d):
        rows = slice(d * SHARD, (d + 1) * SHARD)
        chunks = [absorbed[rows, c * 128 : (c + 1) * 128] for c in range(4)]
        rotary = absorbed[rows, RANK:]
        half = SHARD // 2
        lane = iota((half, 128), 1)
        chunks.append(jnp.where(lane < ROPE, rotary[:half], rotary[half:]))
        return jnp.concatenate(chunks, axis=0)

    major, minor = place(0)
    gathered[0, major * SIDE + minor] = packed(0)
    for d in range(1, SEQ):
        outgoing[d] = packed(d)
    pl.semaphore_wait(barrier, POOL - 1 + TP - 1)
    for d in range(1, SEQ):
        a2a(d).start()

    def gather(i, carry):
        @pl.when(i < SEQ)
        def _():
            @pl.when(i > 0)
            def _():
                a2a(i).wait_recv()

            for j in range(SIDE - 1):
                ag1(i, j).start()

        @pl.when(i > 0)
        def _():
            for j in range(SIDE - 1):
                ag1(i - 1, j).wait_recv()
            for j in range(SIDE - 1):
                ag2(i - 1, j).start()

        return carry

    lax.fori_loop(0, SEQ + 1, gather, 0)

    loads[2].wait()
    row, col = iota((SEQ * STEPS, SEQ * STEPS), 0), iota((SEQ * STEPS, SEQ * STEPS), 1)
    pick = ((col >> 2) == slot_vector(row >> 2)) & ((col & 3) == (row & 3))
    ordered = dot(jnp.where(pick, 1.0, 0.0).astype(BF16), fresh[...]).astype(BF16)
    scores = dot_nt(absorbed[...], ordered) * SCALE
    row, col = iota(scores.shape, 0), iota(scores.shape, 1)
    causal = ((col >> 2) == (row >> 5)) & ((col & 3) <= (row & 3))
    top = jnp.max(jnp.where(causal, scores, MASKED), axis=1, keepdims=True)
    weights = jnp.where(causal, jnp.exp(scores - top), 0.0)
    high = weights.astype(BF16)
    low = (weights - high.astype(F32)).astype(BF16)
    fresh_sums[...] = dot(high, ordered[:, :RANK]) + dot(low, ordered[:, :RANK])
    fresh_stats[...] = two_columns(top, jnp.sum(weights, axis=1, keepdims=True))

    rope_keys[...] = jnp.zeros_like(rope_keys)
    loads[3].wait()
    loads[4].wait()

    def attend(d):
        target = (pool + d) % POOL
        slot = slot_of(pool, target)
        length = lengths[pool, slot]
        start, running = jnp.int32(0), jnp.int32(0)
        for k in range(SEQ):
            other = packing[k]
            start = jnp.where(other == slot, running, start)
            stored = (lengths[pool, other] + ROWS - 1) // ROWS - tp + TP - 1
            running = running + stored // TP
        for c in range(SLOTS):
            index = jnp.minimum(start + c, BLOCKS - 1)
            keys[c * ROWS : (c + 1) * ROWS, :] = latents[index]
            rope_keys[ROPE : 2 * ROPE, c * ROWS : (c + 1) * ROWS] = ropes[index]

        def half(i, carry):
            shards = TP // 2
            rows = shards * SHARD
            part = gathered[d, pl.ds(i * shards, shards)]
            latent_query = jnp.concatenate(
                [part[:, c * SHARD : (c + 1) * SHARD].reshape(rows, 128) for c in range(4)], axis=1
            )
            rope_query = part[:, 4 * SHARD :].reshape(rows // 2, 128)
            upper = dot(rope_query, rope_keys[ROPE : 3 * ROPE]).reshape(shards, SHARD // 2, KEYS)
            lower = dot(rope_query, rope_keys[: 2 * ROPE]).reshape(shards, SHARD // 2, KEYS)
            rotary = jnp.concatenate([upper, lower], axis=1).reshape(rows, KEYS)
            scores = (dot_nt(latent_query, keys[...]) + rotary) * SCALE
            lane = iota((1, KEYS), 1)
            position = ROWS * (tp + TP * (lane >> 7)) + (lane & (ROWS - 1))
            usable = position < length
            top = jnp.max(jnp.where(usable, scores, MASKED), axis=1, keepdims=True)
            weights = jnp.where(usable, jnp.exp(scores - top), 0.0)
            total = jnp.sum(weights, axis=1, keepdims=True)
            sums = dot(weights.astype(BF16), keys[...])
            sums1[d, pl.ds(i * shards, shards)] = sums.astype(BF16).reshape(shards, SHARD, RANK)
            columns = two_columns(top, total)
            for part_index in range(2):
                block = columns[part_index * 128 : (part_index + 1) * 128]
                stats1[d, i * 2 + part_index] = block.T[:8]
            return carry

        lax.fori_loop(0, 2, half, 0)

    def columns_of(first, others):
        rows = [first] + [others[j] for j in range(SIDE - 1)]
        rows.append(jnp.zeros((128 - 8 * SIDE, 128), F32))
        return jnp.concatenate(rows, axis=0).T

    def merge1(d):
        major, minor = place(d % 2)
        columns = columns_of(stats1[d, major], [stats1_in[d, j] for j in range(SIDE - 1)])
        pieces = [sums1[d, pl.ds(major * SIDE, SIDE)]]
        pieces += [sums1_in[d, j] for j in range(SIDE - 1)]
        parts = []
        for j, piece in enumerate(pieces):
            parts.append(
                (
                    piece.reshape(SIDE * SHARD, RANK),
                    columns[:, 8 * j : 8 * j + 1],
                    columns[:, 8 * j + 1 : 8 * j + 2],
                )
            )
        sums, top, total = merge(parts)
        sums2[d] = sums.astype(BF16).reshape(SIDE, SHARD, RANK)
        stats2[d] = two_columns(top, total).T[:8]

    def merge2(d):
        major, minor = place(d % 2)
        columns = columns_of(stats2[d], [stats2_in[d, j] for j in range(SIDE - 1)])
        turned[...] = columns.reshape(SIDE, SHARD, 128)
        columns = turned[minor]
        pieces = [sums2[d, minor]] + [sums2_in[d, j] for j in range(SIDE - 1)]
        parts = []
        for j, piece in enumerate(pieces):
            parts.append((piece, columns[:, 8 * j : 8 * j + 1], columns[:, 8 * j + 1 : 8 * j + 2]))
        sums, top, total = merge(parts)
        return sums.astype(BF16), two_columns(top, total)

    def work(i, carry):
        @pl.when(i < SEQ)
        def _():
            for j in range(SIDE - 1):
                ag2(i, j).wait_recv()
            attend(i)
            for j in range(SIDE - 1):
                for copy in rs1(i, j):
                    copy.start()

        @pl.when((i >= 1) & (i < SEQ + 1))
        def _():
            d = i - 1
            for j in range(SIDE - 1):
                for copy in rs1(d, j):
                    copy.wait_recv()
            merge1(d)
            for j in range(SIDE - 1):
                for copy in rs2(d, j):
                    copy.start()

        @pl.when(i >= 2)
        def _():
            d = i - 2
            for j in range(SIDE - 1):
                for copy in rs2(d, j):
                    copy.wait_recv()
            sums, stats = merge2(d)

            @pl.when(d == 0)
            def _():
                sums3_in[0] = sums
                stats3_in[0] = stats

            @pl.when(d > 0)
            def _():
                sums3[d] = sums
                stats3[d] = stats
                for copy in back(d):
                    copy.start()

        return carry

    lax.fori_loop(0, SEQ + 2, work, 0)

    for d in range(1, SEQ):
        for copy in back(d):
            copy.wait_recv()
    columns = stats3_in[...].reshape(count, 128)
    fresh_columns = fresh_stats[...]
    sums, top, total = merge(
        [
            (sums3_in[...].reshape(count, RANK), columns[:, 0:1], columns[:, 1:2]),
            (fresh_sums[...], fresh_columns[:, 0:1], fresh_columns[:, 1:2]),
        ]
    )
    mixture = (sums / total).astype(BF16)
    for copy in loads[5 : 5 + HEADS]:
        copy.wait()
    values = dot(mixture, uv[...])
    row, lane = iota(values.shape, 0), iota(values.shape, 1)
    values = jnp.where((lane >> 7) == ((row >> 2) & (HEADS - 1)), values, 0.0).astype(BF16)
    row, col = iota((SEQ * STEPS, count), 0), iota((SEQ * STEPS, count), 1)
    pick = ((row >> 2) == slot_vector(col >> 5)) & ((row & 3) == (col & 3))
    values = dot(jnp.where(pick, 1.0, 0.0).astype(BF16), values).astype(BF16)

    def scatter(to):
        return remote(
            part_out.at[to], part_in.at[tp], fin_send.at[to], fin_recv.at[tp], (pool, to)
        )

    def arrive(source):
        return remote(
            part_out.at[source],
            part_in.at[source],
            fin_send.at[source],
            fin_recv.at[source],
            (pool, source),
        )

    half = TP // 2
    loads[5 + HEADS].wait()

    def project(c, carry):
        cols = pl.ds(pl.multiple_of(c * CHUNK, 128), CHUNK)
        part = dot(values, out_weight[:, cols]).astype(BF16)
        for r in range(2):
            to = r * half + c
            part_out[to] = part[r * 16 : (r + 1) * 16]

            @pl.when(to != tp)
            def _():
                scatter(to).start()

        return carry

    lax.fori_loop(0, half, project, 0)
    for j in range(1, TP):
        arrive((tp + j) % TP).wait_recv()
    total = part_out[tp].astype(F32)
    for j in range(1, TP):
        total = total + part_in[(tp + j) % TP].astype(F32)

    def chunk_of(index):
        rows = pl.ds(pl.multiple_of(index // half * 16, 16), 16)
        return out_ref.at[rows, pl.ds(pl.multiple_of(index % half * CHUNK, 128), CHUNK)]

    mine = chunk_of(tp)
    mine[...] = total.astype(BF16)

    def spread_out(to):
        return remote(mine, mine, all_send.at[to], all_recv.at[tp], (pool, to))

    def collect(source):
        piece = chunk_of(source)
        return remote(piece, piece, all_send.at[source], all_recv.at[source], (pool, source))

    for j in range(1, TP):
        spread_out((tp + j) % TP).start()
    for j in range(1, TP):
        collect((tp + j) % TP).wait_recv()

    for j in range(1, TP):
        scatter((tp + j) % TP).wait_send()
        spread_out((tp + j) % TP).wait_send()

    def drain(d, carry):
        for j in range(SIDE - 1):
            ag1(d, j).wait_send()
            ag2(d, j).wait_send()
            for copy in rs1(d, j) + rs2(d, j):
                copy.wait_send()

        @pl.when(d > 0)
        def _():
            a2a(d).wait_send()
            for copy in back(d):
                copy.wait_send()

        return carry

    lax.fori_loop(0, SEQ, drain, 0)


def on_device(
    queries,
    new_rows,
    prefill_latent,
    prefill_rope,
    lengths,
    owner,
    pack_order,
    uk_weight,
    uv_weight,
    out_weight,
):
    rows = SEQ * STEPS
    fresh = jnp.pad(new_rows.reshape(rows, RANK + ROPE), ((0, 0), (0, 128 - ROPE)))
    dma = pltpu.SemaphoreType.DMA
    anywhere = pl.BlockSpec(memory_space=pl.ANY)
    scalars = pl.BlockSpec(memory_space=pltpu.SMEM)
    out = pl.pallas_call(
        kernel,
        out_shape=jax.ShapeDtypeStruct((rows, WIDTH), BF16),
        in_specs=[scalars] * 3 + [anywhere] * 7,
        out_specs=pl.BlockSpec(memory_space=pltpu.VMEM),
        scratch_shapes=[
            pltpu.VMEM((rows, HEADS * (NOPE + ROPE)), BF16),
            pltpu.VMEM((rows, RANK + 128), BF16),
            pltpu.VMEM((BLOCKS, ROWS, RANK), BF16),
            pltpu.VMEM((BLOCKS, ROPE, ROWS), BF16),
            pltpu.VMEM((HEADS, NOPE, RANK), BF16),
            pltpu.VMEM((RANK, HEADS * 128), BF16),
            pltpu.VMEM((HEADS * 128, WIDTH), BF16),
            pltpu.VMEM((HEADS * (NOPE + ROPE), RANK + 128), BF16),
            pltpu.VMEM((SEQ * SHARD, RANK + 128), BF16),
            pltpu.VMEM((SEQ, PACK, 128), BF16),
            pltpu.VMEM((SEQ, TP, PACK, 128), BF16),
            pltpu.VMEM((KEYS, RANK), BF16),
            pltpu.VMEM((3 * ROPE, KEYS), BF16),
            pltpu.VMEM((SEQ, TP, SHARD, RANK), BF16),
            pltpu.VMEM((SEQ, SIDE, 8, 128), F32),
            pltpu.VMEM((SEQ, SIDE - 1, SIDE, SHARD, RANK), BF16),
            pltpu.VMEM((SEQ, SIDE - 1, 8, 128), F32),
            pltpu.VMEM((SEQ, SIDE, SHARD, RANK), BF16),
            pltpu.VMEM((SEQ, 8, 128), F32),
            pltpu.VMEM((SEQ, SIDE - 1, SHARD, RANK), BF16),
            pltpu.VMEM((SEQ, SIDE - 1, 8, 128), F32),
            pltpu.VMEM((SIDE, SHARD, 128), F32),
            pltpu.VMEM((SEQ, SHARD, RANK), BF16),
            pltpu.VMEM((SEQ, SHARD, 128), F32),
            pltpu.VMEM((SEQ, SHARD, RANK), BF16),
            pltpu.VMEM((SEQ, SHARD, 128), F32),
            pltpu.VMEM((SEQ * SHARD, RANK), F32),
            pltpu.VMEM((SEQ * SHARD, 128), F32),
            pltpu.VMEM((TP, 16, CHUNK), BF16),
            pltpu.VMEM((TP, 16, CHUNK), BF16),
            dma((6 + HEADS,)),
        ]
        + [dma((SEQ,))] * 2
        + [dma((SEQ, SIDE - 1))] * 12
        + [dma((SEQ,))] * 4
        + [dma((TP,))] * 4,
        compiler_params=pltpu.CompilerParams(
            collective_id=0, has_side_effects=True, vmem_limit_bytes=60 << 20
        ),
    )(
        owner,
        lengths,
        pack_order.reshape(SEQ),
        queries.reshape(rows, HEADS * (NOPE + ROPE)),
        fresh,
        prefill_latent.reshape(BLOCKS, ROWS, RANK),
        prefill_rope.reshape(BLOCKS, ROPE, ROWS),
        uk_weight,
        uv_weight,
        out_weight,
    )
    return out.reshape(SEQ, STEPS, WIDTH)


def solution(mesh):
    placed = (
        P("pool", None, "tp"),
        P("pool", None, None),
        P("pool", "tp", None, None, None),
        P("pool", "tp", None, None, None),
        P(),
        P(),
        P("pool", "tp", None),
        P("tp", None, None),
        P("tp", None, None),
        P("tp", None),
    )
    return jax.shard_map(
        on_device, mesh=mesh, in_specs=placed, out_specs=P("pool", None, None), check_vma=False
    )
```

```python
import jax
import jax.numpy as jnp
from jax import lax
from jax.experimental import pallas as pl
from jax.experimental.pallas import tpu as pltpu
from jax.sharding import PartitionSpec as P

MESH = pl.DeviceIdType.MESH
F32 = jnp.float32
BF16 = jnp.bfloat16
MASKED = -1e30

POOL = 8
SIDE = 4
TP = 16
SEQ = 8
STEPS = 4
HEADS = 8
NOPE = 128
ROPE = 64
RANK = 512
BLOCKS = 44
ROWS = 128
SLOTS = 8
KEYS = SLOTS * ROWS
SHARD = HEADS * STEPS
PACK = SHARD * 4 + SHARD // 2
WIDTH = 7168
CHUNK = 896
SCALE = (NOPE + ROPE) ** -0.5
PARTS = 4
AHEAD1, AHEAD2, AHEAD3 = 5, 3, 1
BEHIND0, BEHIND1, BEHIND2 = 1, 2, 3


def iota(shape, dim):
    return lax.broadcasted_iota(jnp.int32, shape, dim)


def dot(a, b):
    return jnp.dot(a, b, preferred_element_type=F32)


def dot_nt(a, b):
    return lax.dot_general(a, b, (((1,), (1,)), ((), ())), preferred_element_type=F32)


def two_columns(first, second):
    lane = iota((first.shape[0], 128), 1)
    return jnp.where(lane == 0, first, jnp.where(lane == 1, second, 0.0))


def merge(parts):
    top = parts[0][1]
    for part in parts[1:]:
        top = jnp.maximum(top, part[1])
    sums, totals = 0.0, 0.0
    for part in parts:
        factor = jnp.exp(part[1] - top)
        sums = sums + factor * part[0].astype(F32)
        totals = totals + factor * part[2]
    return sums, top, totals


def kernel(
    owner,
    lengths,
    packing,
    queries_hbm,
    fresh_hbm,
    latent_hbm,
    rope_hbm,
    uk_hbm,
    uv_hbm,
    out_weight_hbm,
    out_ref,
    queries,
    fresh,
    flat_queries,
    flat_fresh,
    latents,
    ropes,
    uk,
    uv,
    out_weight,
    wide,
    absorbed,
    outgoing,
    gathered,
    keys,
    rope_keys,
    sums1,
    stats1,
    sums0_in,
    stats0_in,
    sums1_in,
    stats1_in,
    sums2,
    stats2,
    sums2_in,
    stats2_in,
    turned,
    fresh_sums,
    fresh_stats,
    mixture,
    part_out,
    part_in,
    local_sem,
    a2a_send,
    a2a_recv,
    ag1_send,
    ag1_recv,
    ret_send,
    ret_recv,
    rets_send,
    rets_recv,
    ag2_send,
    ag2_recv,
    ag3_send,
    ag3_recv,
    rs0_send,
    rs0_recv,
    rs0s_send,
    rs0s_recv,
    rs1_send,
    rs1_recv,
    rs1s_send,
    rs1s_recv,
    fin_send,
    fin_recv,
    all_send,
    all_recv,
):
    pool = lax.axis_index("pool")
    tp = lax.axis_index("tp")
    z, x = tp // SIDE, tp % SIDE

    def place(par):
        return z + par * (x - z), x + par * (z - x)

    def minor_peer(par, j):
        major, minor = place(par)
        to = (minor + j) % SIDE
        return to, (pool, (1 - par) * (z * SIDE + to) + par * (to * SIDE + x))

    def major_peer(par, j):
        major, minor = place(par)
        to = (major + j) % SIDE
        return to, (pool, (1 - par) * (to * SIDE + x) + par * (z * SIDE + to))

    def remote(source, target, send, recv, device):
        return pltpu.make_async_remote_copy(
            src_ref=source,
            dst_ref=target,
            send_sem=send,
            recv_sem=recv,
            device_id=device,
            device_id_type=MESH,
        )

    def load(index, source, target):
        return pltpu.make_async_copy(source, target, local_sem.at[index])

    loads = [
        load(0, queries_hbm, queries),
        load(1, uk_hbm, uk),
        load(2, fresh_hbm, fresh),
    ]
    for copy in loads:
        copy.start()

    def cache_loads(part):
        piece = pl.ds(part * (BLOCKS // PARTS), BLOCKS // PARTS)
        return (
            load(3 + part, latent_hbm.at[piece], latents.at[piece]),
            load(3 + PARTS + part, rope_hbm.at[piece], ropes.at[piece]),
        )

    def weight_loads(h):
        piece = pl.ds(pl.multiple_of(h * 128, 128), 128)
        return (
            load(3 + 2 * PARTS + h, uv_hbm.at[h], uv.at[:, piece]),
            load(3 + 2 * PARTS + HEADS + h, out_weight_hbm.at[piece], out_weight.at[piece]),
        )

    barrier = pltpu.get_barrier_semaphore()
    for d in range(1, POOL):
        for j in range(SIDE):
            device = ((pool + d) % POOL, minor_peer(d % 2, j)[1][1])
            pl.semaphore_signal(barrier, inc=1, device_id=device, device_id_type=MESH)
    for j in range(1, TP):
        pl.semaphore_signal(barrier, inc=1, device_id=(pool, (tp + j) % TP), device_id_type=MESH)

    def slot_of(s, g):
        slot = jnp.int32(0)
        for k in range(1, SEQ):
            slot = jnp.where(owner[s, k] == g, k, slot)
        return slot

    slots = [slot_of((pool + POOL - d) % POOL, pool) for d in range(SEQ)]

    def slot_vector(which):
        vector = jnp.zeros(which.shape, jnp.int32)
        for d in range(SEQ):
            vector = jnp.where(which == d, slots[d], vector)
        return vector

    wide[...] = jnp.zeros_like(wide)
    row, lane = iota((ROPE, 128), 0), iota((ROPE, 128), 1)
    unit = jnp.where((lane & (ROPE - 1)) == row, 1.0, 0.0).astype(BF16)
    for h in range(HEADS):
        start = h * (NOPE + ROPE)
        wide[start + NOPE : start + NOPE + ROPE, RANK:] = unit
    loads[1].wait()
    for h in range(HEADS):
        start = h * (NOPE + ROPE)
        wide[start : start + NOPE, :RANK] = uk[h]
    count = SEQ * SHARD
    row, col = iota((count, SEQ * STEPS), 0), iota((count, SEQ * STEPS), 1)
    pick = ((col >> 2) == slot_vector(row >> 5)) & ((col & 3) == (row & 3))
    loads[0].wait()
    for k in range(SEQ):
        flat_queries[k * STEPS : (k + 1) * STEPS] = queries[k].astype(F32)
    spread = dot(jnp.where(pick, 1.0, 0.0).astype(BF16), flat_queries[...].astype(BF16))
    row, lane = iota(spread.shape, 0), iota(spread.shape, 1)
    first = ((row >> 2) & (HEADS - 1)) * (NOPE + ROPE)
    spread = jnp.where((lane >= first) & (lane < first + NOPE + ROPE), spread, 0.0)
    absorbed[...] = dot(spread.astype(BF16), wide[...]).astype(BF16)

    def a2a(d):
        major, minor = place(d % 2)
        return remote(
            outgoing.at[d],
            gathered.at[d, major * SIDE + minor],
            a2a_send.at[d],
            a2a_recv.at[d],
            ((pool + POOL - d) % POOL, tp),
        )

    def ag1(d, j):
        major, minor = place(d % 2)
        piece = gathered.at[d, major * SIDE + minor]
        return remote(
            piece, piece, ag1_send.at[d, j], ag1_recv.at[d, j], minor_peer(d % 2, j)[1]
        )

    def ag2(d, side):
        major, minor = place(d % 2)
        piece = gathered.at[d, pl.ds(major * SIDE, SIDE)]
        return remote(
            piece,
            piece,
            ag2_send.at[d, side],
            ag2_recv.at[d, side],
            major_peer(d % 2, 1 + 2 * side)[1],
        )

    def ag3(d, side):
        origin = major_peer(d % 2, 3 - 2 * side)[0]
        piece = gathered.at[d, pl.ds(origin * SIDE + 2 * side, 2)]
        return remote(
            piece,
            piece,
            ag3_send.at[d, side],
            ag3_recv.at[d, side],
            major_peer(d % 2, 1 + 2 * side)[1],
        )

    def rs0(d, side):
        opposite = major_peer(d % 2, 2)[0]
        device = major_peer(d % 2, 1 + 2 * side)[1]
        return (
            remote(
                sums1.at[d, pl.ds(opposite * SIDE + 2 * side, 2)],
                sums0_in.at[d, side],
                rs0_send.at[d, side],
                rs0_recv.at[d, side],
                device,
            ),
            remote(
                stats1.at[d, opposite],
                stats0_in.at[d, side],
                rs0s_send.at[d, side],
                rs0s_recv.at[d, side],
                device,
            ),
        )

    def rs1(d, side):
        to, device = major_peer(d % 2, 1 + 2 * side)
        return (
            remote(
                sums1.at[d, pl.ds(to * SIDE, SIDE)],
                sums1_in.at[d, side],
                rs1_send.at[d, side],
                rs1_recv.at[d, side],
                device,
            ),
            remote(
                stats1.at[d, to],
                stats1_in.at[d, side],
                rs1s_send.at[d, side],
                rs1s_recv.at[d, side],
                device,
            ),
        )

    def back(d, j):
        to, device = minor_peer(d % 2, j)
        device = ((pool + d) % POOL, device[1])
        return (
            remote(
                sums2.at[d, to],
                sums2_in.at[d, j],
                ret_send.at[d, j],
                ret_recv.at[d, j],
                device,
            ),
            remote(
                stats2.at[d],
                stats2_in.at[d, j],
                rets_send.at[d, j],
                rets_recv.at[d, j],
                device,
            ),
        )

    def each_way(d, body):
        for j in range(1, SIDE):
            body(j)

        @pl.when(d > 0)
        def _():
            body(0)

    def packed(d):
        rows = slice(d * SHARD, (d + 1) * SHARD)
        chunks = [absorbed[rows, c * 128 : (c + 1) * 128] for c in range(4)]
        rotary = absorbed[rows, RANK:]
        half = SHARD // 2
        lane = iota((half, 128), 1)
        chunks.append(jnp.where(lane < ROPE, rotary[:half], rotary[half:]))
        return jnp.concatenate(chunks, axis=0)

    major, minor = place(0)
    gathered[0, major * SIDE + minor] = packed(0)
    for d in range(1, SEQ):
        outgoing[d] = packed(d)
    pl.semaphore_wait(barrier, (POOL - 1) * SIDE + TP - 1)
    for d in range(1, SEQ):
        a2a(d).start()

    def stage(d, body):
        @pl.when((d >= 0) & (d < SEQ))
        def _():
            body(d)

    def first_gather(d):
        @pl.when(d > 0)
        def _():
            a2a(d).wait_recv()

        for j in range(1, SIDE):
            ag1(d, j).start()

    def second_gather(d):
        for j in range(1, SIDE):
            ag1(d, j).wait_recv()
        for side in range(2):
            ag2(d, side).start()

    def third_gather(d):
        for side in range(2):
            ag2(d, side).wait_recv()
            ag3(d, side).start()

    def early(i, carry):
        stage(i + AHEAD1, first_gather)
        stage(i + AHEAD2, second_gather)
        stage(i + AHEAD3, third_gather)

        @pl.when(i + AHEAD1 < PARTS)
        def _():
            for copy in cache_loads(i + AHEAD1):
                copy.start()

        return carry

    lax.fori_loop(-AHEAD1, 0, early, 0)

    loads[2].wait()
    row, col = iota((SEQ * STEPS, SEQ * STEPS), 0), iota((SEQ * STEPS, SEQ * STEPS), 1)
    pick = ((col >> 2) == slot_vector(row >> 2)) & ((col & 3) == (row & 3))
    flat_fresh[...] = jnp.zeros_like(flat_fresh)
    for k in range(SEQ):
        flat_fresh[k * STEPS : (k + 1) * STEPS, : RANK + ROPE] = fresh[k].astype(F32)
    flat = flat_fresh[...].astype(BF16)
    ordered = dot(jnp.where(pick, 1.0, 0.0).astype(BF16), flat).astype(BF16)
    scores = dot_nt(absorbed[...], ordered) * SCALE
    row, col = iota(scores.shape, 0), iota(scores.shape, 1)
    causal = ((col >> 2) == (row >> 5)) & ((col & 3) <= (row & 3))
    top = jnp.max(jnp.where(causal, scores, MASKED), axis=1, keepdims=True)
    weights = jnp.where(causal, jnp.exp(scores - top), 0.0)
    high = weights.astype(BF16)
    low = (weights - high.astype(F32)).astype(BF16)
    sums = dot(high, ordered[:, :RANK]) + dot(low, ordered[:, :RANK])
    fresh_sums[...] = sums.reshape(SEQ, SHARD, RANK)
    columns = two_columns(top, jnp.sum(weights, axis=1, keepdims=True))
    fresh_stats[...] = columns.reshape(SEQ, SHARD, 128)

    rope_keys[...] = jnp.zeros_like(rope_keys)
    for part in range(PARTS):
        for copy in cache_loads(part):
            copy.wait()

    def attend(d):
        target = (pool + d) % POOL
        slot = slot_of(pool, target)
        length = lengths[pool, slot]
        start, running = jnp.int32(0), jnp.int32(0)
        for k in range(SEQ):
            other = packing[k]
            start = jnp.where(other == slot, running, start)
            stored = (lengths[pool, other] + ROWS - 1) // ROWS - tp + TP - 1
            running = running + stored // TP
        for c in range(SLOTS):
            index = jnp.minimum(start + c, BLOCKS - 1)
            keys[c * ROWS : (c + 1) * ROWS, :] = latents[index]
            rope_keys[ROPE : 2 * ROPE, c * ROWS : (c + 1) * ROWS] = ropes[index]

        def half(i, carry):
            shards = TP // 2
            rows = shards * SHARD
            part = gathered[d, pl.ds(i * shards, shards)]
            latent_query = jnp.concatenate(
                [part[:, c * SHARD : (c + 1) * SHARD].reshape(rows, 128) for c in range(4)], axis=1
            )
            rope_query = part[:, 4 * SHARD :].reshape(rows // 2, 128)
            upper = dot(rope_query, rope_keys[ROPE : 3 * ROPE]).reshape(shards, SHARD // 2, KEYS)
            lower = dot(rope_query, rope_keys[: 2 * ROPE]).reshape(shards, SHARD // 2, KEYS)
            rotary = jnp.concatenate([upper, lower], axis=1).reshape(rows, KEYS)
            scores = (dot_nt(latent_query, keys[...]) + rotary) * SCALE
            lane = iota((1, KEYS), 1)
            position = ROWS * (tp + TP * (lane >> 7)) + (lane & (ROWS - 1))
            usable = position < length
            top = jnp.max(jnp.where(usable, scores, MASKED), axis=1, keepdims=True)
            weights = jnp.where(usable, jnp.exp(scores - top), 0.0)
            total = jnp.sum(weights, axis=1, keepdims=True)
            sums = dot(weights.astype(BF16), keys[...])
            sums1[d, pl.ds(i * shards, shards)] = sums.astype(BF16).reshape(shards, SHARD, RANK)
            columns = two_columns(top, total)
            for part_index in range(2):
                block = columns[part_index * 128 : (part_index + 1) * 128]
                stats1[d, i * 2 + part_index] = block.T[:8]
            return carry

        lax.fori_loop(0, 2, half, 0)

    def columns_of(rows):
        rows = rows + [jnp.zeros((128 - 8 * len(rows), 128), F32)]
        return jnp.concatenate(rows, axis=0).T

    def merge0(d):
        nexts = [major_peer(d % 2, 1 + 2 * side)[0] for side in range(2)]
        columns = columns_of(
            [stats1[d, to] for to in nexts] + [stats0_in[d, side] for side in range(2)]
        )
        rows = 2 * SHARD
        halves = []
        for side, to in enumerate(nexts):
            half = slice(side * rows, (side + 1) * rows)
            piece = pl.ds(to * SIDE + 2 * side, 2)
            parts = []
            for index, sums in ((side, sums1[d, piece]), (side + 2, sums0_in[d, side])):
                parts.append(
                    (
                        sums.reshape(rows, RANK),
                        columns[half, 8 * index : 8 * index + 1],
                        columns[half, 8 * index + 1 : 8 * index + 2],
                    )
                )
            sums, top, total = merge(parts)
            sums1[d, piece] = sums.astype(BF16).reshape(2, SHARD, RANK)
            halves.append((top, total))
        first = jnp.concatenate([two_columns(*halves[0]), columns[rows:]], axis=0)
        stats1[d, nexts[0]] = first.T[:8]
        kept = two_columns(columns[:rows, 8:9], columns[:rows, 9:10])
        stats1[d, nexts[1]] = jnp.concatenate([kept, two_columns(*halves[1])], axis=0).T[:8]

    def merge1(d):
        major, minor = place(d % 2)
        columns = columns_of([stats1[d, major]] + [stats1_in[d, side] for side in range(2)])
        pieces = [sums1[d, pl.ds(major * SIDE, SIDE)]]
        pieces += [sums1_in[d, side] for side in range(2)]
        parts = []
        for j, piece in enumerate(pieces):
            parts.append(
                (
                    piece.reshape(SIDE * SHARD, RANK),
                    columns[:, 8 * j : 8 * j + 1],
                    columns[:, 8 * j + 1 : 8 * j + 2],
                )
            )
        sums, top, total = merge(parts)
        sums2[d] = sums.astype(BF16).reshape(SIDE, SHARD, RANK)
        stats2[d] = two_columns(top, total).T[:8]

        @pl.when(d == 0)
        def _():
            sums2_in[0, 0] = sums2[0, minor]
            stats2_in[0, 0] = stats2[0]

    def merge2(d):
        major, minor = place(d % 2)
        columns = columns_of([stats2_in[d, j] for j in range(SIDE)])
        turned[...] = columns.reshape(SIDE, SHARD, 128)
        columns = turned[minor]
        fresh_columns = fresh_stats[d]
        parts = [(fresh_sums[d], fresh_columns[:, 0:1], fresh_columns[:, 1:2])]
        for j in range(SIDE):
            parts.append(
                (
                    sums2_in[d, j],
                    columns[:, 8 * j : 8 * j + 1],
                    columns[:, 8 * j + 1 : 8 * j + 2],
                )
            )
        sums, top, total = merge(parts)
        mixture[d] = (sums / total).astype(BF16)

    def middle(d):
        for side in range(2):
            ag3(d, side).wait_recv()
        attend(d)
        for side in range(2):
            for copy in rs0(d, side):
                copy.start()

    def passing(d):
        for side in range(2):
            for copy in rs0(d, side):
                copy.wait_recv()
        merge0(d)
        for side in range(2):
            for copy in rs1(d, side):
                copy.start()

    def first_scatter(d):
        for side in range(2):
            for copy in rs1(d, side):
                copy.wait_recv()
        merge1(d)

        def send(j):
            for copy in back(d, j):
                copy.start()

        each_way(d, send)

    def finish(d):
        def wait(j):
            for copy in back(d, j):
                copy.wait_recv()

        each_way(d, wait)
        merge2(d)

    def start_weights(h):
        for copy in weight_loads(h):
            copy.start()

    def work(i, carry):
        stage(i, start_weights)
        stage(i + AHEAD1, first_gather)
        stage(i + AHEAD2, second_gather)
        stage(i + AHEAD3, third_gather)
        stage(i, middle)
        stage(i - BEHIND0, passing)
        stage(i - BEHIND1, first_scatter)
        stage(i - BEHIND2, finish)
        return carry

    lax.fori_loop(0, SEQ + BEHIND2, work, 0)

    for h in range(HEADS):
        for copy in weight_loads(h):
            copy.wait()
    values = dot(mixture[...].reshape(count, RANK), uv[...])
    row, lane = iota(values.shape, 0), iota(values.shape, 1)
    values = jnp.where((lane >> 7) == ((row >> 2) & (HEADS - 1)), values, 0.0).astype(BF16)
    row, col = iota((SEQ * STEPS, count), 0), iota((SEQ * STEPS, count), 1)
    pick = ((row >> 2) == slot_vector(col >> 5)) & ((row & 3) == (col & 3))
    values = dot(jnp.where(pick, 1.0, 0.0).astype(BF16), values).astype(BF16)

    def scatter(to):
        return remote(
            part_out.at[to], part_in.at[tp], fin_send.at[to], fin_recv.at[tp], (pool, to)
        )

    def arrive(source):
        return remote(
            part_out.at[source],
            part_in.at[source],
            fin_send.at[source],
            fin_recv.at[source],
            (pool, source),
        )

    half = TP // 2

    def project(c, carry):
        cols = pl.ds(pl.multiple_of(c * CHUNK, 128), CHUNK)
        part = dot(values, out_weight[:, cols]).astype(BF16)
        for r in range(2):
            to = r * half + c
            part_out[to] = part[r * 16 : (r + 1) * 16]

            @pl.when(to != tp)
            def _():
                scatter(to).start()

        return carry

    lax.fori_loop(0, half, project, 0)
    for j in range(1, TP):
        arrive((tp + j) % TP).wait_recv()
    total = part_out[tp].astype(F32)
    for j in range(1, TP):
        total = total + part_in[(tp + j) % TP].astype(F32)

    def chunk_of(index):
        rows = pl.ds(pl.multiple_of(index // half * 16, 16), 16)
        return out_ref.at[rows, pl.ds(pl.multiple_of(index % half * CHUNK, 128), CHUNK)]

    mine = chunk_of(tp)
    mine[...] = total.astype(BF16)

    def spread_out(to):
        return remote(mine, mine, all_send.at[to], all_recv.at[tp], (pool, to))

    def collect(source):
        piece = chunk_of(source)
        return remote(piece, piece, all_send.at[source], all_recv.at[source], (pool, source))

    for j in range(1, TP):
        spread_out((tp + j) % TP).start()
    for j in range(1, TP):
        collect((tp + j) % TP).wait_recv()

    for j in range(1, TP):
        scatter((tp + j) % TP).wait_send()
        spread_out((tp + j) % TP).wait_send()

    def drain(d, carry):
        for j in range(1, SIDE):
            ag1(d, j).wait_send()

        @pl.when(d > 0)
        def _():
            a2a(d).wait_send()

        def sent(j):
            for copy in back(d, j):
                copy.wait_send()

        each_way(d, sent)
        for side in range(2):
            ag2(d, side).wait_send()
            ag3(d, side).wait_send()
            for copy in rs0(d, side) + rs1(d, side):
                copy.wait_send()

        return carry

    lax.fori_loop(0, SEQ, drain, 0)


def on_device(
    queries,
    new_rows,
    prefill_latent,
    prefill_rope,
    lengths,
    owner,
    pack_order,
    uk_weight,
    uv_weight,
    out_weight,
):
    rows = SEQ * STEPS
    dma = pltpu.SemaphoreType.DMA
    anywhere = pl.BlockSpec(memory_space=pl.ANY)
    scalars = pl.BlockSpec(memory_space=pltpu.SMEM)
    out = pl.pallas_call(
        kernel,
        out_shape=jax.ShapeDtypeStruct((rows, WIDTH), BF16),
        in_specs=[scalars] * 3 + [anywhere] * 7,
        out_specs=pl.BlockSpec(memory_space=pltpu.VMEM),
        scratch_shapes=[
            pltpu.VMEM((SEQ, STEPS, HEADS * (NOPE + ROPE)), BF16),
            pltpu.VMEM((SEQ, STEPS, RANK + ROPE), BF16),
            pltpu.VMEM((rows, HEADS * (NOPE + ROPE)), F32),
            pltpu.VMEM((rows, RANK + 128), F32),
            pltpu.VMEM((BLOCKS, ROWS, RANK), BF16),
            pltpu.VMEM((BLOCKS, ROPE, ROWS), BF16),
            pltpu.VMEM((HEADS, NOPE, RANK), BF16),
            pltpu.VMEM((RANK, HEADS * 128), BF16),
            pltpu.VMEM((HEADS * 128, WIDTH), BF16),
            pltpu.VMEM((HEADS * (NOPE + ROPE), RANK + 128), BF16),
            pltpu.VMEM((SEQ * SHARD, RANK + 128), BF16),
            pltpu.VMEM((SEQ, PACK, 128), BF16),
            pltpu.VMEM((SEQ, TP, PACK, 128), BF16),
            pltpu.VMEM((KEYS, RANK), BF16),
            pltpu.VMEM((3 * ROPE, KEYS), BF16),
            pltpu.VMEM((SEQ, TP, SHARD, RANK), BF16),
            pltpu.VMEM((SEQ, SIDE, 8, 128), F32),
            pltpu.VMEM((SEQ, 2, 2, SHARD, RANK), BF16),
            pltpu.VMEM((SEQ, 2, 8, 128), F32),
            pltpu.VMEM((SEQ, 2, SIDE, SHARD, RANK), BF16),
            pltpu.VMEM((SEQ, 2, 8, 128), F32),
            pltpu.VMEM((SEQ, SIDE, SHARD, RANK), BF16),
            pltpu.VMEM((SEQ, 8, 128), F32),
            pltpu.VMEM((SEQ, SIDE, SHARD, RANK), BF16),
            pltpu.VMEM((SEQ, SIDE, 8, 128), F32),
            pltpu.VMEM((SIDE, SHARD, 128), F32),
            pltpu.VMEM((SEQ, SHARD, RANK), F32),
            pltpu.VMEM((SEQ, SHARD, 128), F32),
            pltpu.VMEM((SEQ, SHARD, RANK), BF16),
            pltpu.VMEM((TP, 16, CHUNK), BF16),
            pltpu.VMEM((TP, 16, CHUNK), BF16),
            dma((3 + 2 * PARTS + 2 * HEADS,)),
        ]
        + [dma((SEQ,))] * 2
        + [dma((SEQ, SIDE))] * 6
        + [dma((SEQ, 2))] * 12
        + [dma((TP,))] * 4,
        compiler_params=pltpu.CompilerParams(
            collective_id=0, has_side_effects=True, vmem_limit_bytes=60 << 20
        ),
    )(
        owner,
        lengths,
        pack_order.reshape(SEQ),
        queries,
        new_rows,
        prefill_latent.reshape(BLOCKS, ROWS, RANK),
        prefill_rope.reshape(BLOCKS, ROPE, ROWS),
        uk_weight,
        uv_weight,
        out_weight,
    )
    return out.reshape(SEQ, STEPS, WIDTH)


def solution(mesh):
    placed = (
        P("pool", None, "tp"),
        P("pool", None, None),
        P("pool", "tp", None, None, None),
        P("pool", "tp", None, None, None),
        P(),
        P(),
        P("pool", "tp", None),
        P("tp", None, None),
        P("tp", None, None),
        P("tp", None),
    )
    return jax.shard_map(
        on_device, mesh=mesh, in_specs=placed, out_specs=P("pool", None, None), check_vma=False
    )
```

```python
import jax
import jax.numpy as jnp
from jax import lax
from jax.experimental import pallas as pl
from jax.experimental.pallas import tpu as pltpu
from jax.sharding import PartitionSpec as P

MESH = pl.DeviceIdType.MESH
F32 = jnp.float32
BF16 = jnp.bfloat16
MASKED = -1e30

POOL = 8
SIDE = 4
TP = 16
SEQ = 8
STEPS = 4
HEADS = 8
NOPE = 128
ROPE = 64
RANK = 512
BLOCKS = 44
ROWS = 128
SLOTS = 8
KEYS = SLOTS * ROWS
SHARD = HEADS * STEPS
PACK = SHARD * 4 + SHARD // 2
WIDTH = 7168
CHUNK = 896
SCALE = (NOPE + ROPE) ** -0.5
PARTS = 4
AHEAD1, AHEAD2, AHEAD3 = 5, 4, 1
BEHIND0, BEHIND1, BEHIND2 = 1, 3, 5


def iota(shape, dim):
    return lax.broadcasted_iota(jnp.int32, shape, dim)


def dot(a, b):
    return jnp.dot(a, b, preferred_element_type=F32)


def dot_nt(a, b):
    return lax.dot_general(a, b, (((1,), (1,)), ((), ())), preferred_element_type=F32)


def two_columns(first, second):
    lane = iota((first.shape[0], 128), 1)
    return jnp.where(lane == 0, first, jnp.where(lane == 1, second, 0.0))


def merge(parts):
    top = parts[0][1]
    for part in parts[1:]:
        top = jnp.maximum(top, part[1])
    sums, totals = 0.0, 0.0
    for part in parts:
        factor = jnp.exp(part[1] - top)
        sums = sums + factor * part[0].astype(F32)
        totals = totals + factor * part[2]
    return sums, top, totals


def kernel(
    owner,
    lengths,
    packing,
    queries_hbm,
    fresh_hbm,
    latent_hbm,
    rope_hbm,
    uk_hbm,
    uv_hbm,
    out_weight_hbm,
    out_ref,
    queries,
    fresh,
    flat_queries,
    flat_fresh,
    latents,
    ropes,
    uk,
    uv,
    out_weight,
    wide,
    absorbed,
    outgoing,
    gathered,
    keys,
    rope_keys,
    sums1,
    stats1,
    sums0_in,
    stats0_in,
    sums1_in,
    stats1_in,
    sums2,
    stats2,
    sums2_in,
    stats2_in,
    turned,
    fresh_sums,
    fresh_stats,
    mixture,
    part_out,
    part_in,
    local_sem,
    a2a_send,
    a2a_recv,
    ag1_send,
    ag1_recv,
    ret_send,
    ret_recv,
    rets_send,
    rets_recv,
    ag2_send,
    ag2_recv,
    ag3_send,
    ag3_recv,
    rs0_send,
    rs0_recv,
    rs0s_send,
    rs0s_recv,
    rs1_send,
    rs1_recv,
    rs1s_send,
    rs1s_recv,
    fin_send,
    fin_recv,
    all_send,
    all_recv,
):
    pool = lax.axis_index("pool")
    tp = lax.axis_index("tp")
    z, x = tp // SIDE, tp % SIDE

    def place(par):
        return z + par * (x - z), x + par * (z - x)

    def minor_peer(par, j):
        major, minor = place(par)
        to = (minor + j) % SIDE
        return to, (pool, (1 - par) * (z * SIDE + to) + par * (to * SIDE + x))

    def major_peer(par, j):
        major, minor = place(par)
        to = (major + j) % SIDE
        return to, (pool, (1 - par) * (to * SIDE + x) + par * (z * SIDE + to))

    def remote(source, target, send, recv, device):
        return pltpu.make_async_remote_copy(
            src_ref=source,
            dst_ref=target,
            send_sem=send,
            recv_sem=recv,
            device_id=device,
            device_id_type=MESH,
        )

    def load(index, source, target):
        return pltpu.make_async_copy(source, target, local_sem.at[index])

    loads = [
        load(0, queries_hbm, queries),
        load(1, uk_hbm, uk),
        load(2, fresh_hbm, fresh),
    ]
    for copy in loads:
        copy.start()

    def cache_loads(part):
        piece = pl.ds(part * (BLOCKS // PARTS), BLOCKS // PARTS)
        return (
            load(3 + part, latent_hbm.at[piece], latents.at[piece]),
            load(3 + PARTS + part, rope_hbm.at[piece], ropes.at[piece]),
        )

    def weight_loads(h):
        piece = pl.ds(pl.multiple_of(h * 128, 128), 128)
        return (
            load(3 + 2 * PARTS + h, uv_hbm.at[h], uv.at[:, piece]),
            load(3 + 2 * PARTS + HEADS + h, out_weight_hbm.at[piece], out_weight.at[piece]),
        )

    barrier = pltpu.get_barrier_semaphore()
    for d in range(1, POOL):
        for j in range(SIDE):
            device = ((pool + d) % POOL, minor_peer(d % 2, j)[1][1])
            pl.semaphore_signal(barrier, inc=1, device_id=device, device_id_type=MESH)
    for j in range(1, TP):
        pl.semaphore_signal(barrier, inc=1, device_id=(pool, (tp + j) % TP), device_id_type=MESH)

    def slot_of(s, g):
        slot = jnp.int32(0)
        for k in range(1, SEQ):
            slot = jnp.where(owner[s, k] == g, k, slot)
        return slot

    slots = [slot_of((pool + POOL - d) % POOL, pool) for d in range(SEQ)]

    def slot_vector(which):
        vector = jnp.zeros(which.shape, jnp.int32)
        for d in range(SEQ):
            vector = jnp.where(which == d, slots[d], vector)
        return vector

    wide[...] = jnp.zeros_like(wide)
    row, lane = iota((ROPE, 128), 0), iota((ROPE, 128), 1)
    unit = jnp.where((lane & (ROPE - 1)) == row, 1.0, 0.0).astype(BF16)
    for h in range(HEADS):
        start = h * (NOPE + ROPE)
        wide[start + NOPE : start + NOPE + ROPE, RANK:] = unit
    loads[1].wait()
    for h in range(HEADS):
        start = h * (NOPE + ROPE)
        wide[start : start + NOPE, :RANK] = uk[h]
    count = SEQ * SHARD
    row, col = iota((count, SEQ * STEPS), 0), iota((count, SEQ * STEPS), 1)
    pick = ((col >> 2) == slot_vector(row >> 5)) & ((col & 3) == (row & 3))
    loads[0].wait()
    for k in range(SEQ):
        flat_queries[k * STEPS : (k + 1) * STEPS] = queries[k].astype(F32)
    spread = dot(jnp.where(pick, 1.0, 0.0).astype(BF16), flat_queries[...].astype(BF16))
    row, lane = iota(spread.shape, 0), iota(spread.shape, 1)
    first = ((row >> 2) & (HEADS - 1)) * (NOPE + ROPE)
    spread = jnp.where((lane >= first) & (lane < first + NOPE + ROPE), spread, 0.0)
    absorbed[...] = dot(spread.astype(BF16), wide[...]).astype(BF16)

    def a2a(d):
        major, minor = place(d % 2)
        return remote(
            outgoing.at[d],
            gathered.at[d, major * SIDE + minor],
            a2a_send.at[d],
            a2a_recv.at[d],
            ((pool + POOL - d) % POOL, tp),
        )

    def ag1(d, j):
        major, minor = place(d % 2)
        piece = gathered.at[d, major * SIDE + minor]
        return remote(
            piece, piece, ag1_send.at[d, j], ag1_recv.at[d, j], minor_peer(d % 2, j)[1]
        )

    def ag2(d, side):
        major, minor = place(d % 2)
        piece = gathered.at[d, pl.ds(major * SIDE, SIDE)]
        return remote(
            piece,
            piece,
            ag2_send.at[d, side],
            ag2_recv.at[d, side],
            major_peer(d % 2, 1 + 2 * side)[1],
        )

    def ag3(d, side):
        origin = major_peer(d % 2, 3 - 2 * side)[0]
        piece = gathered.at[d, pl.ds(origin * SIDE + 2 * side, 2)]
        return remote(
            piece,
            piece,
            ag3_send.at[d, side],
            ag3_recv.at[d, side],
            major_peer(d % 2, 1 + 2 * side)[1],
        )

    def rs0(d, side):
        opposite = major_peer(d % 2, 2)[0]
        device = major_peer(d % 2, 1 + 2 * side)[1]
        return (
            remote(
                sums1.at[d, pl.ds(opposite * SIDE + 2 * side, 2)],
                sums0_in.at[d, side],
                rs0_send.at[d, side],
                rs0_recv.at[d, side],
                device,
            ),
            remote(
                stats1.at[d, opposite],
                stats0_in.at[d, side],
                rs0s_send.at[d, side],
                rs0s_recv.at[d, side],
                device,
            ),
        )

    def rs1(d, side):
        to, device = major_peer(d % 2, 1 + 2 * side)
        return (
            remote(
                sums1.at[d, pl.ds(to * SIDE, SIDE)],
                sums1_in.at[d, side],
                rs1_send.at[d, side],
                rs1_recv.at[d, side],
                device,
            ),
            remote(
                stats1.at[d, to],
                stats1_in.at[d, side],
                rs1s_send.at[d, side],
                rs1s_recv.at[d, side],
                device,
            ),
        )

    def back(d, j):
        to, device = minor_peer(d % 2, j)
        device = ((pool + d) % POOL, device[1])
        return (
            remote(
                sums2.at[d, to],
                sums2_in.at[d, j],
                ret_send.at[d, j],
                ret_recv.at[d, j],
                device,
            ),
            remote(
                stats2.at[d],
                stats2_in.at[d, j],
                rets_send.at[d, j],
                rets_recv.at[d, j],
                device,
            ),
        )

    def each_way(d, body):
        for j in range(1, SIDE):
            body(j)

        @pl.when(d > 0)
        def _():
            body(0)

    def packed(d):
        rows = slice(d * SHARD, (d + 1) * SHARD)
        chunks = [absorbed[rows, c * 128 : (c + 1) * 128] for c in range(4)]
        rotary = absorbed[rows, RANK:]
        half = SHARD // 2
        lane = iota((half, 128), 1)
        chunks.append(jnp.where(lane < ROPE, rotary[:half], rotary[half:]))
        return jnp.concatenate(chunks, axis=0)

    major, minor = place(0)
    gathered[0, major * SIDE + minor] = packed(0)
    for d in range(1, SEQ):
        outgoing[d] = packed(d)
    pl.semaphore_wait(barrier, (POOL - 1) * SIDE + TP - 1)
    for d in range(1, SEQ):
        a2a(d).start()

    def stage(d, body):
        @pl.when((d >= 0) & (d < SEQ))
        def _():
            body(d)

    def first_gather(d):
        @pl.when(d > 0)
        def _():
            a2a(d).wait_recv()

        for j in range(1, SIDE):
            ag1(d, j).start()

    def second_gather(d):
        for j in range(1, SIDE):
            ag1(d, j).wait_recv()
        for side in range(2):
            ag2(d, side).start()

    def third_gather(d):
        for side in range(2):
            ag2(d, side).wait_recv()
            ag3(d, side).start()

    def early(i, carry):
        stage(i + AHEAD1, first_gather)
        stage(i + AHEAD2, second_gather)
        stage(i + AHEAD3, third_gather)

        @pl.when(i + AHEAD1 < PARTS)
        def _():
            for copy in cache_loads(i + AHEAD1):
                copy.start()

        return carry

    lax.fori_loop(-AHEAD1, 0, early, 0)

    loads[2].wait()
    row, col = iota((SEQ * STEPS, SEQ * STEPS), 0), iota((SEQ * STEPS, SEQ * STEPS), 1)
    pick = ((col >> 2) == slot_vector(row >> 2)) & ((col & 3) == (row & 3))
    flat_fresh[...] = jnp.zeros_like(flat_fresh)
    for k in range(SEQ):
        flat_fresh[k * STEPS : (k + 1) * STEPS, : RANK + ROPE] = fresh[k].astype(F32)
    flat = flat_fresh[...].astype(BF16)
    ordered = dot(jnp.where(pick, 1.0, 0.0).astype(BF16), flat).astype(BF16)
    scores = dot_nt(absorbed[...], ordered) * SCALE
    row, col = iota(scores.shape, 0), iota(scores.shape, 1)
    causal = ((col >> 2) == (row >> 5)) & ((col & 3) <= (row & 3))
    top = jnp.max(jnp.where(causal, scores, MASKED), axis=1, keepdims=True)
    weights = jnp.where(causal, jnp.exp(scores - top), 0.0)
    high = weights.astype(BF16)
    low = (weights - high.astype(F32)).astype(BF16)
    sums = dot(high, ordered[:, :RANK]) + dot(low, ordered[:, :RANK])
    fresh_sums[...] = sums.reshape(SEQ, SHARD, RANK)
    columns = two_columns(top, jnp.sum(weights, axis=1, keepdims=True))
    fresh_stats[...] = columns.reshape(SEQ, SHARD, 128)

    rope_keys[...] = jnp.zeros_like(rope_keys)
    for part in range(PARTS):
        for copy in cache_loads(part):
            copy.wait()

    def attend(d):
        target = (pool + d) % POOL
        slot = slot_of(pool, target)
        length = lengths[pool, slot]
        start, running = jnp.int32(0), jnp.int32(0)
        for k in range(SEQ):
            other = packing[k]
            start = jnp.where(other == slot, running, start)
            stored = (lengths[pool, other] + ROWS - 1) // ROWS - tp + TP - 1
            running = running + stored // TP
        for c in range(SLOTS):
            index = jnp.minimum(start + c, BLOCKS - 1)
            keys[c * ROWS : (c + 1) * ROWS, :] = latents[index]
            rope_keys[ROPE : 2 * ROPE, c * ROWS : (c + 1) * ROWS] = ropes[index]

        def half(i, carry):
            shards = TP // 2
            rows = shards * SHARD
            part = gathered[d, pl.ds(i * shards, shards)]
            latent_query = jnp.concatenate(
                [part[:, c * SHARD : (c + 1) * SHARD].reshape(rows, 128) for c in range(4)], axis=1
            )
            rope_query = part[:, 4 * SHARD :].reshape(rows // 2, 128)
            upper = dot(rope_query, rope_keys[ROPE : 3 * ROPE]).reshape(shards, SHARD // 2, KEYS)
            lower = dot(rope_query, rope_keys[: 2 * ROPE]).reshape(shards, SHARD // 2, KEYS)
            rotary = jnp.concatenate([upper, lower], axis=1).reshape(rows, KEYS)
            scores = (dot_nt(latent_query, keys[...]) + rotary) * SCALE
            lane = iota((1, KEYS), 1)
            position = ROWS * (tp + TP * (lane >> 7)) + (lane & (ROWS - 1))
            usable = position < length
            top = jnp.max(jnp.where(usable, scores, MASKED), axis=1, keepdims=True)
            weights = jnp.where(usable, jnp.exp(scores - top), 0.0)
            total = jnp.sum(weights, axis=1, keepdims=True)
            sums = dot(weights.astype(BF16), keys[...])
            sums1[d, pl.ds(i * shards, shards)] = sums.astype(BF16).reshape(shards, SHARD, RANK)
            columns = two_columns(top, total)
            for part_index in range(2):
                block = columns[part_index * 128 : (part_index + 1) * 128]
                stats1[d, i * 2 + part_index] = block.T[:8]
            return carry

        lax.fori_loop(0, 2, half, 0, unroll=True)

    def columns_of(rows):
        rows = rows + [jnp.zeros((128 - 8 * len(rows), 128), F32)]
        return jnp.concatenate(rows, axis=0).T

    def merge0(d):
        nexts = [major_peer(d % 2, 1 + 2 * side)[0] for side in range(2)]
        columns = columns_of(
            [stats1[d, to] for to in nexts] + [stats0_in[d, side] for side in range(2)]
        )
        rows = 2 * SHARD
        halves = []
        for side, to in enumerate(nexts):
            half = slice(side * rows, (side + 1) * rows)
            piece = pl.ds(to * SIDE + 2 * side, 2)
            parts = []
            for index, sums in ((side, sums1[d, piece]), (side + 2, sums0_in[d, side])):
                parts.append(
                    (
                        sums.reshape(rows, RANK),
                        columns[half, 8 * index : 8 * index + 1],
                        columns[half, 8 * index + 1 : 8 * index + 2],
                    )
                )
            sums, top, total = merge(parts)
            sums1[d, piece] = sums.astype(BF16).reshape(2, SHARD, RANK)
            halves.append((top, total))
        first = jnp.concatenate([two_columns(*halves[0]), columns[rows:]], axis=0)
        stats1[d, nexts[0]] = first.T[:8]
        kept = two_columns(columns[:rows, 8:9], columns[:rows, 9:10])
        stats1[d, nexts[1]] = jnp.concatenate([kept, two_columns(*halves[1])], axis=0).T[:8]

    def merge1(d):
        major, minor = place(d % 2)
        columns = columns_of([stats1[d, major]] + [stats1_in[d, side] for side in range(2)])
        pieces = [sums1[d, pl.ds(major * SIDE, SIDE)]]
        pieces += [sums1_in[d, side] for side in range(2)]
        parts = []
        for j, piece in enumerate(pieces):
            parts.append(
                (
                    piece.reshape(SIDE * SHARD, RANK),
                    columns[:, 8 * j : 8 * j + 1],
                    columns[:, 8 * j + 1 : 8 * j + 2],
                )
            )
        sums, top, total = merge(parts)
        sums2[d] = sums.astype(BF16).reshape(SIDE, SHARD, RANK)
        stats2[d] = two_columns(top, total).T[:8]

        @pl.when(d == 0)
        def _():
            sums2_in[0, 0] = sums2[0, minor]
            stats2_in[0, 0] = stats2[0]

    def merge2(d):
        major, minor = place(d % 2)
        columns = columns_of([stats2_in[d, j] for j in range(SIDE)])
        turned[...] = columns.reshape(SIDE, SHARD, 128)
        columns = turned[minor]
        fresh_columns = fresh_stats[d]
        parts = [(fresh_sums[d], fresh_columns[:, 0:1], fresh_columns[:, 1:2])]
        for j in range(SIDE):
            parts.append(
                (
                    sums2_in[d, j],
                    columns[:, 8 * j : 8 * j + 1],
                    columns[:, 8 * j + 1 : 8 * j + 2],
                )
            )
        sums, top, total = merge(parts)
        mixture[d] = (sums / total).astype(BF16)

    def middle(d):
        for side in range(2):
            ag3(d, side).wait_recv()
        attend(d)
        for side in range(2):
            for copy in rs0(d, side):
                copy.start()

    def passing(d):
        for side in range(2):
            for copy in rs0(d, side):
                copy.wait_recv()
        merge0(d)
        for side in range(2):
            for copy in rs1(d, side):
                copy.start()

    def first_scatter(d):
        for side in range(2):
            for copy in rs1(d, side):
                copy.wait_recv()
        merge1(d)

        def send(j):
            for copy in back(d, j):
                copy.start()

        each_way(d, send)

    def finish(d):
        def wait(j):
            for copy in back(d, j):
                copy.wait_recv()

        each_way(d, wait)
        merge2(d)

    def start_weights(h):
        for copy in weight_loads(h):
            copy.start()

    def work(i, carry):
        stage(i, start_weights)
        stage(i + AHEAD1, first_gather)
        stage(i + AHEAD2, second_gather)
        stage(i + AHEAD3, third_gather)
        stage(i, middle)
        stage(i - BEHIND0, passing)
        stage(i - BEHIND1, first_scatter)
        stage(i - BEHIND2, finish)
        return carry

    lax.fori_loop(0, SEQ + BEHIND2, work, 0)

    for h in range(HEADS):
        for copy in weight_loads(h):
            copy.wait()
    values = dot(mixture[...].reshape(count, RANK), uv[...])
    row, lane = iota(values.shape, 0), iota(values.shape, 1)
    values = jnp.where((lane >> 7) == ((row >> 2) & (HEADS - 1)), values, 0.0).astype(BF16)
    row, col = iota((SEQ * STEPS, count), 0), iota((SEQ * STEPS, count), 1)
    pick = ((row >> 2) == slot_vector(col >> 5)) & ((row & 3) == (col & 3))
    values = dot(jnp.where(pick, 1.0, 0.0).astype(BF16), values).astype(BF16)

    def scatter(to):
        return remote(
            part_out.at[to], part_in.at[tp], fin_send.at[to], fin_recv.at[tp], (pool, to)
        )

    def arrive(source):
        return remote(
            part_out.at[source],
            part_in.at[source],
            fin_send.at[source],
            fin_recv.at[source],
            (pool, source),
        )

    half = TP // 2

    def project(c, carry):
        cols = pl.ds(pl.multiple_of(c * CHUNK, 128), CHUNK)
        part = dot(values, out_weight[:, cols]).astype(BF16)
        for r in range(2):
            to = r * half + c
            part_out[to] = part[r * 16 : (r + 1) * 16]

            @pl.when(to != tp)
            def _():
                scatter(to).start()

        return carry

    lax.fori_loop(0, half, project, 0)
    for j in range(1, TP):
        arrive((tp + j) % TP).wait_recv()
    total = part_out[tp].astype(F32)
    for j in range(1, TP):
        total = total + part_in[(tp + j) % TP].astype(F32)

    def chunk_of(index):
        rows = pl.ds(pl.multiple_of(index // half * 16, 16), 16)
        return out_ref.at[rows, pl.ds(pl.multiple_of(index % half * CHUNK, 128), CHUNK)]

    mine = chunk_of(tp)
    mine[...] = total.astype(BF16)

    def spread_out(to):
        return remote(mine, mine, all_send.at[to], all_recv.at[tp], (pool, to))

    def collect(source):
        piece = chunk_of(source)
        return remote(piece, piece, all_send.at[source], all_recv.at[source], (pool, source))

    for j in range(1, TP):
        spread_out((tp + j) % TP).start()

    def drain(d, carry):
        for j in range(1, SIDE):
            ag1(d, j).wait_send()

        @pl.when(d > 0)
        def _():
            a2a(d).wait_send()

        def sent(j):
            for copy in back(d, j):
                copy.wait_send()

        each_way(d, sent)
        for side in range(2):
            ag2(d, side).wait_send()
            ag3(d, side).wait_send()
            for copy in rs0(d, side) + rs1(d, side):
                copy.wait_send()

        return carry

    lax.fori_loop(0, SEQ, drain, 0)
    for j in range(1, TP):
        scatter((tp + j) % TP).wait_send()
    for j in range(1, TP):
        collect((tp + j) % TP).wait_recv()
    for j in range(1, TP):
        spread_out((tp + j) % TP).wait_send()


def on_device(
    queries,
    new_rows,
    prefill_latent,
    prefill_rope,
    lengths,
    owner,
    pack_order,
    uk_weight,
    uv_weight,
    out_weight,
):
    rows = SEQ * STEPS
    dma = pltpu.SemaphoreType.DMA
    anywhere = pl.BlockSpec(memory_space=pl.ANY)
    scalars = pl.BlockSpec(memory_space=pltpu.SMEM)
    out = pl.pallas_call(
        kernel,
        out_shape=jax.ShapeDtypeStruct((rows, WIDTH), BF16),
        in_specs=[scalars] * 3 + [anywhere] * 7,
        out_specs=pl.BlockSpec(memory_space=pltpu.VMEM),
        scratch_shapes=[
            pltpu.VMEM((SEQ, STEPS, HEADS * (NOPE + ROPE)), BF16),
            pltpu.VMEM((SEQ, STEPS, RANK + ROPE), BF16),
            pltpu.VMEM((rows, HEADS * (NOPE + ROPE)), F32),
            pltpu.VMEM((rows, RANK + 128), F32),
            pltpu.VMEM((BLOCKS, ROWS, RANK), BF16),
            pltpu.VMEM((BLOCKS, ROPE, ROWS), BF16),
            pltpu.VMEM((HEADS, NOPE, RANK), BF16),
            pltpu.VMEM((RANK, HEADS * 128), BF16),
            pltpu.VMEM((HEADS * 128, WIDTH), BF16),
            pltpu.VMEM((HEADS * (NOPE + ROPE), RANK + 128), BF16),
            pltpu.VMEM((SEQ * SHARD, RANK + 128), BF16),
            pltpu.VMEM((SEQ, PACK, 128), BF16),
            pltpu.VMEM((SEQ, TP, PACK, 128), BF16),
            pltpu.VMEM((KEYS, RANK), BF16),
            pltpu.VMEM((3 * ROPE, KEYS), BF16),
            pltpu.VMEM((SEQ, TP, SHARD, RANK), BF16),
            pltpu.VMEM((SEQ, SIDE, 8, 128), F32),
            pltpu.VMEM((SEQ, 2, 2, SHARD, RANK), BF16),
            pltpu.VMEM((SEQ, 2, 8, 128), F32),
            pltpu.VMEM((SEQ, 2, SIDE, SHARD, RANK), BF16),
            pltpu.VMEM((SEQ, 2, 8, 128), F32),
            pltpu.VMEM((SEQ, SIDE, SHARD, RANK), BF16),
            pltpu.VMEM((SEQ, 8, 128), F32),
            pltpu.VMEM((SEQ, SIDE, SHARD, RANK), BF16),
            pltpu.VMEM((SEQ, SIDE, 8, 128), F32),
            pltpu.VMEM((SIDE, SHARD, 128), F32),
            pltpu.VMEM((SEQ, SHARD, RANK), F32),
            pltpu.VMEM((SEQ, SHARD, 128), F32),
            pltpu.VMEM((SEQ, SHARD, RANK), BF16),
            pltpu.VMEM((TP, 16, CHUNK), BF16),
            pltpu.VMEM((TP, 16, CHUNK), BF16),
            dma((3 + 2 * PARTS + 2 * HEADS,)),
        ]
        + [dma((SEQ,))] * 2
        + [dma((SEQ, SIDE))] * 6
        + [dma((SEQ, 2))] * 12
        + [dma((TP,))] * 4,
        compiler_params=pltpu.CompilerParams(
            collective_id=0, has_side_effects=True, vmem_limit_bytes=60 << 20
        ),
    )(
        owner,
        lengths,
        pack_order.reshape(SEQ),
        queries,
        new_rows,
        prefill_latent.reshape(BLOCKS, ROWS, RANK),
        prefill_rope.reshape(BLOCKS, ROPE, ROWS),
        uk_weight,
        uv_weight,
        out_weight,
    )
    return out.reshape(SEQ, STEPS, WIDTH)


def solution(mesh):
    placed = (
        P("pool", None, "tp"),
        P("pool", None, None),
        P("pool", "tp", None, None, None),
        P("pool", "tp", None, None, None),
        P(),
        P(),
        P("pool", "tp", None),
        P("tp", None, None),
        P("tp", None, None),
        P("tp", None),
    )
    return jax.shard_map(
        on_device, mesh=mesh, in_specs=placed, out_specs=P("pool", None, None), check_vma=False
    )
```
